32 devices in a mesh: cp: 4 (over y, x), ep: 8 (over z, core).
Axes of the slice: x: 2, y: 2, z: 4, core: 2. Of those that a mesh axis runs over, the one named last changes fastest.
Arguments:
- tokens: bfloat16 [8, 256, 3584], P('ep', 'cp'), may hold values from -6 to 6
- cotangent: bfloat16 [8, 256, 3584], P('ep', 'cp'), may hold values from -6 to 6
- routes: int32 [8, 256, 8], P('ep', 'cp'), may hold values from 0 to 31, all different within a row; in each aligned block of 64 rows (0 to 63, 64 to 127, ..., all dimensions but the last counted through in order) at most 20 rows name the same one
- router_weights: float32 [8, 256, 8], P('ep', 'cp'), may hold values from 0.02 to 0.5
- w_gate: bfloat16 [32, 3584, 1024], P(('cp', 'ep')), may hold values from -0.09375 to 0.09375
- w_up: bfloat16 [32, 3584, 1024], P(('cp', 'ep')), may hold values from -0.09375 to 0.09375
- w_down: bfloat16 [32, 1024, 3584], P(('cp', 'ep')), may hold values from -0.1875 to 0.1875
Outputs:
- layer_out: bfloat16 [8, 256, 3584], P('ep', 'cp')
- token_grad: bfloat16 [8, 256, 3584], P('ep', 'cp')
- gate_grad: float32 [8, 256, 8], P('ep', 'cp')
The draws below stay inside these ranges and needn't reach their ends.
Inputs may be any that keep to these rules, and one draw needn't show every extreme that they name: `routes`: each row names 8 distinct experts; in each aligned block of 64 rows (the rows of one device) no expert is named by more than 20 of the block's slots.
All inputs are finite; a program needn't handle non-finite values.
Results may differ from the reference program's by a relative error of at most 0.0058.
Values may be sent and summed in bfloat16 or wider, within the bound.
A program may use at most 128 MiB of HBM per device.

```python
import math
import jax
import jax.numpy as jnp
import numpy as np
from jax import lax

D = 3584
FF = 1024
TOP = 8
SEQ_DEV = 64
LEN = 256
EXPERTS = 32
MOST = 20
N_EP = 8


def block_scale(own_key, extent, pieces, smallest, high):
    gain = 1.0
    for axis_at, parts in pieces:
        steps = jax.random.uniform(jax.random.fold_in(jax.random.fold_in(own_key, 6), axis_at), (parts,), jnp.float32, smallest / len(pieces), high / len(pieces))
        gain = gain * jnp.repeat(jnp.exp(steps), extent[axis_at] // parts).reshape((-1,) + (1,) * (len(extent) - 1 - axis_at))
    return gain


def shared_out(stream_key, own, number, rows, number_of, top, bound, lean):
    order = jax.random.permutation(stream_key, number_of)
    crowded, common = portions_of(number_of, rows * top, bound, lean, True), portions_of(number_of, rows * top, bound, lean, False)
    places = jnp.arange(number_of)

    def named(lengths, rotation):
        used = int((lengths > 0).sum())
        fixed = max(1, used // 4)
        moved = fixed + (places - fixed + rotation * (used - fixed)) % max(1, number_of - fixed)
        return jnp.zeros((number_of,), jnp.int32).at[order[jnp.where(places < fixed, places, moved)]].set(jnp.asarray(lengths, jnp.int32))

    lengths = jnp.where(number % 4 == 0, named(crowded, number // 4), named(common, number - number // 4 - 1))
    mixed = jax.random.permutation(jax.random.fold_in(own, 3), number_of)
    source_of, sink = mixed[0:number_of // 2 * 2:2], mixed[1:number_of // 2 * 2:2]
    room = jnp.minimum(lengths[source_of] - 1, bound - lengths[sink]) // 2
    room = jnp.where((source_of == order[0]) | (sink == order[0]) | (lengths[sink] == 0), 0, jnp.maximum(room, 0))
    moved = jax.random.randint(jax.random.fold_in(own, 4), (number_of // 2,), 0, 1 << 20) % (room + 1)
    lengths = lengths.at[source_of].add(-moved).at[sink].add(moved)
    members = jnp.searchsorted(jnp.cumsum(lengths), jnp.arange(rows * top), side="right").astype(jnp.int32)
    listing = members.reshape(top, rows).T
    listing = listing[jax.random.permutation(jax.random.fold_in(own, 1), rows)]
    rotation = jax.random.randint(jax.random.fold_in(own, 2), (rows, 1), 0, top)
    return jnp.take_along_axis(listing, (jnp.arange(top)[None, :] + rotation) % top, axis=1)


def portions_of(amount, total, limit, lean, full):
    portions = [(1 << 20) // math.isqrt(grade ** lean) + 1 for grade in range(1, amount + 1)]
    largest = limit if full else min(limit, max(-(-total // amount), total * portions[0] // sum(portions)))
    least = 1 if total - largest >= amount - 1 else 0
    given, surplus = [largest] + [least] * (amount - 1), total - largest - least * (amount - 1)
    while surplus > 0:
        free = [i for i in range(1, amount) if given[i] < largest] or [i for i in range(1, amount) if given[i] < limit]
        pool, left = sum([portions[i] for i in free]), surplus
        for i in free:
            extra = min(limit - given[i], max(1, left * portions[i] // pool), surplus)
            given[i] = given[i] + extra
            surplus = surplus - extra
    return np.array(given)


def bell_draw(stream_key, dims, deviation, limit, cuts=(), held_as=jnp.bfloat16):
    level = block_scale(stream_key, dims, cuts, -0.22, 0.18) if cuts else 1.0
    drawn = jax.random.normal(stream_key, dims, jnp.float32) * deviation * level
    return jnp.minimum(jnp.maximum(drawn, -limit), limit).astype(held_as)


def setup_inputs(seed: int = 0) -> dict:
    arg_keys = jax.random.split(jax.random.key(seed), 8)
    tokens = bell_draw(arg_keys[0], (N_EP, LEN, D), 1.0, 6.0, ((0, 8), (1, 4)))
    cotangent = bell_draw(arg_keys[1], (N_EP, LEN, D), 1.0, 6.0, ((0, 8), (1, 4)))
    routes_keys = jax.random.split(jax.random.fold_in(arg_keys[2], 1), N_EP * LEN // SEQ_DEV)
    routes_turns = jax.random.permutation(jax.random.fold_in(arg_keys[2], 3), N_EP * LEN // SEQ_DEV)
    routes = jax.vmap(lambda own, number: shared_out(jax.random.fold_in(arg_keys[2], 2), own, number, SEQ_DEV, EXPERTS, TOP, MOST, 2))(routes_keys, routes_turns).reshape((N_EP, LEN, TOP))
    router_weights = jnp.clip(jnp.exp(math.log(0.5) - 3.218876 * jax.random.uniform(arg_keys[3], (N_EP, LEN, TOP), jnp.float32) ** block_scale(arg_keys[3], (N_EP, LEN, TOP), ((0, 8), (1, 4)), -0.2, 0.2)), 0.02, 0.5)
    w_gate = bell_draw(arg_keys[4], (EXPERTS, D, FF), D ** -0.5, 0.09375, ((0, 32),))
    w_up = bell_draw(arg_keys[5], (EXPERTS, D, FF), D ** -0.5, 0.09375, ((0, 32),))
    w_down = bell_draw(arg_keys[6], (EXPERTS, FF, D), FF ** -0.5, 0.1875, ((0, 32),))
    return dict(tokens=tokens, cotangent=cotangent, routes=routes, router_weights=router_weights, w_gate=w_gate, w_up=w_up, w_down=w_down)


def expert_rows(inputs, grad_in, gate_matrix, up_matrix, down_matrix):
    gate_pre = jnp.dot(inputs, gate_matrix, preferred_element_type=jnp.float32)
    up_pre = jnp.dot(inputs, up_matrix, preferred_element_type=jnp.float32)
    sig_gate = jax.nn.sigmoid(gate_pre)
    silu_gate = gate_pre * sig_gate
    hidden = (silu_gate * up_pre).astype(jnp.bfloat16)
    expert_out = jnp.dot(hidden, down_matrix, preferred_element_type=jnp.float32).astype(jnp.bfloat16)
    grad_hidden = jnp.dot(grad_in, down_matrix.T, preferred_element_type=jnp.float32)
    grad_gate = (grad_hidden * up_pre * sig_gate * (1.0 + gate_pre * (1.0 - sig_gate))).astype(jnp.bfloat16)
    grad_up = (grad_hidden * silu_gate).astype(jnp.bfloat16)
    expert_grad = (jnp.dot(grad_gate, gate_matrix.T, preferred_element_type=jnp.float32)
                   + jnp.dot(grad_up, up_matrix.T, preferred_element_type=jnp.float32)).astype(jnp.bfloat16)
    return expert_out, expert_grad


def reference(tokens, cotangent, routes, router_weights, w_gate, w_up, w_down):
    total = N_EP * LEN
    padded_tokens = jnp.concatenate([tokens.reshape(total, D), jnp.zeros((1, D), jnp.bfloat16)], 0)
    padded_cot = jnp.concatenate([cotangent.reshape(total, D), jnp.zeros((1, D), jnp.bfloat16)], 0)
    flat_routes = routes.reshape(total * TOP)
    flat_mix = jnp.concatenate([router_weights.reshape(total * TOP), jnp.zeros((1,), jnp.float32)], 0)
    capacity = EXPERTS * MOST

    def visit(expert, carry):
        out_acc, grad_acc, gate_acc = carry
        slot_index = jnp.nonzero(flat_routes == expert, size=capacity, fill_value=total * TOP)[0].astype(jnp.int32)
        token_index = (slot_index // TOP).astype(jnp.int32)
        inputs = padded_tokens[token_index]
        grad_in = padded_cot[token_index]
        gate_matrix = lax.dynamic_index_in_dim(w_gate, expert, 0, keepdims=False)
        up_matrix = lax.dynamic_index_in_dim(w_up, expert, 0, keepdims=False)
        down_matrix = lax.dynamic_index_in_dim(w_down, expert, 0, keepdims=False)
        expert_out, expert_grad = expert_rows(inputs, grad_in, gate_matrix, up_matrix, down_matrix)
        mixing = flat_mix[slot_index]
        out_f = expert_out.astype(jnp.float32)
        out_acc = out_acc.at[token_index].add(mixing[:, None] * out_f)
        grad_acc = grad_acc.at[token_index].add(mixing[:, None] * expert_grad.astype(jnp.float32))
        gate_acc = gate_acc.at[slot_index].add(jnp.sum(grad_in.astype(jnp.float32) * out_f, -1))
        return out_acc, grad_acc, gate_acc

    start = (jnp.zeros((total + 1, D), jnp.float32), jnp.zeros((total + 1, D), jnp.float32),
             jnp.zeros((total * TOP + 1,), jnp.float32))
    out_acc, grad_acc, gate_acc = lax.fori_loop(0, EXPERTS, visit, start)
    layer_out = out_acc[:total].astype(jnp.bfloat16).reshape(N_EP, LEN, D)
    token_grad = grad_acc[:total].astype(jnp.bfloat16).reshape(N_EP, LEN, D)
    gate_grad = gate_acc[:total * TOP].reshape(N_EP, LEN, TOP)
    return (layer_out, token_grad, gate_grad)
```

```python
import jax
import jax.numpy as jnp
from jax import lax
from jax.sharding import PartitionSpec as P

F32 = jnp.float32
BF16 = jnp.bfloat16


def dot(a, b, contract=(1, 0)):
    return lax.dot_general(
        a, b, (((contract[0],), (contract[1],)), ((), ())), preferred_element_type=F32
    )


def per_device(tokens, cotangent, routes, router_weights, w_gate, w_up, w_down):
    cp_count = lax.axis_size("cp")
    ep_count = lax.axis_size("ep")
    owners = cp_count * ep_count
    positions = tokens.shape[1]
    features = tokens.shape[2]
    top_k = routes.shape[2]
    capacity = positions * top_k // owners * 5 // 4
    part = ep_count * capacity
    everyone = ep_count * positions
    my_cp = lax.axis_index("cp")
    my_ep = lax.axis_index("ep")
    gate_matrix = w_gate[0]
    up_matrix = w_up[0]
    down_matrix = w_down[0]

    meta = jnp.concatenate([routes[0].astype(F32), router_weights[0]], axis=1)
    meta = lax.all_gather(meta, "ep", axis=0, tiled=False)
    tok_all = lax.all_gather(tokens[0], "ep", axis=0, tiled=True)
    cot_all = lax.all_gather(cotangent[0], "ep", axis=0, tiled=True)

    def partner(step):
        return lax.rem(my_cp + step, cp_count)

    def out_to(step, value):
        return lax.ppermute(value, "cp", [(c, (c + step) % cp_count) for c in range(cp_count)])

    def back_from(step, value):
        return lax.ppermute(value, "cp", [((c + step) % cp_count, c) for c in range(cp_count)])

    all_routes = meta[:, :, :top_k].astype(jnp.int32)
    all_weights = meta[:, :, top_k:]
    earlier = (jnp.arange(positions)[:, None] < jnp.arange(positions)[None, :]).astype(F32)
    names, slots, weights = [], [], []
    for step in range(cp_count):
        expert = partner(step) * ep_count + my_ep
        named = all_routes == expert
        named_any = jnp.any(named, axis=2)
        rank = dot(named_any.astype(F32), earlier).astype(jnp.int32)
        base = jnp.arange(ep_count, dtype=jnp.int32)[:, None] * capacity
        slots.append(jnp.where(named_any, base + rank, -1).reshape(1, everyone))
        weights.append(jnp.sum(jnp.where(named, all_weights, 0.0), axis=2).reshape(everyone, 1))
        names.append(named)
    row_ids = jnp.arange(part, dtype=jnp.int32)
    pick = [row_ids[:, None] == slot for slot in slots]

    def dispatch(dense):
        packed = [dot(p.astype(BF16), dense).astype(BF16) for p in pick]
        arrived = [packed[0]] + [out_to(s, packed[s]) for s in range(1, cp_count)]
        return packed, jnp.concatenate(arrived, axis=0)

    _, inputs = dispatch(tok_all)
    cot_packed, grad_in = dispatch(cot_all)

    gate_pre = dot(inputs, gate_matrix)
    up_pre = dot(inputs, up_matrix)
    sig_gate = jax.nn.sigmoid(gate_pre)
    silu_gate = gate_pre * sig_gate
    hidden = (silu_gate * up_pre).astype(BF16)
    expert_out = dot(hidden, down_matrix).astype(BF16)

    spread = []
    for step in range(cp_count):
        here = row_ids[None, :] == slots[step].reshape(everyone, 1)
        spread.append(jnp.where(here, weights[step], 0.0))
    spread = jnp.concatenate(spread, axis=1)
    spread_hi = lax.reduce_precision(spread, 8, 7)
    spread_lo = (spread - spread_hi).astype(BF16)
    spread_hi = spread_hi.astype(BF16)

    def bring_back(rows):
        pieces = [rows[s * part:(s + 1) * part] for s in range(cp_count)]
        return [pieces[0]] + [back_from(s, pieces[s]) for s in range(1, cp_count)]

    def combine(pieces):
        rows = jnp.concatenate(pieces, axis=0)
        dense = (dot(spread_hi, rows) + dot(spread_lo, rows)).astype(BF16)
        return lax.psum_scatter(dense, "ep", scatter_dimension=0, tiled=True)

    out_pieces = bring_back(expert_out)

    grad_hidden = dot(grad_in, down_matrix, (1, 1))
    grad_gate = (grad_hidden * up_pre * sig_gate * (1.0 + gate_pre * (1.0 - sig_gate))).astype(BF16)
    grad_up = (grad_hidden * silu_gate).astype(BF16)
    expert_grad = (
        dot(grad_gate, gate_matrix, (1, 1)) + dot(grad_up, up_matrix, (1, 1))
    ).astype(BF16)
    grad_pieces = bring_back(expert_grad)

    layer_out = combine(out_pieces)
    gate_parts = jnp.zeros((ep_count, positions, top_k), F32)
    for step in range(cp_count):
        scores = jnp.sum(
            cot_packed[step].astype(F32) * out_pieces[step].astype(F32), axis=1, keepdims=True
        )
        by_token = jnp.sum(jnp.where(pick[step], scores, 0.0), axis=0)
        gate_parts += jnp.where(names[step], by_token.reshape(ep_count, positions, 1), 0.0)
    gate_grad = lax.psum_scatter(gate_parts, "ep", scatter_dimension=0, tiled=False)
    token_grad = combine(grad_pieces)
    return layer_out[None], token_grad[None], gate_grad[None]


def solution(mesh):
    in_specs = (
        P("ep", "cp", None),
        P("ep", "cp", None),
        P("ep", "cp", None),
        P("ep", "cp", None),
        P(("cp", "ep"), None, None),
        P(("cp", "ep"), None, None),
        P(("cp", "ep"), None, None),
    )
    out_specs = (P("ep", "cp", None), P("ep", "cp", None), P("ep", "cp", None))
    return jax.shard_map(
        per_device, mesh=mesh, in_specs=in_specs, out_specs=out_specs, check_vma=False
    )
```

```python
import jax
import jax.numpy as jnp
from jax import lax
from jax.sharding import PartitionSpec as P

F32 = jnp.float32
BF16 = jnp.bfloat16


def dot(a, b, contract=(1, 0)):
    return lax.dot_general(
        a, b, (((contract[0],), (contract[1],)), ((), ())), preferred_element_type=F32
    )


def per_device(tokens, cotangent, routes, router_weights, w_gate, w_up, w_down):
    cp_count = lax.axis_size("cp")
    ep_count = lax.axis_size("ep")
    owners = cp_count * ep_count
    positions = tokens.shape[1]
    features = tokens.shape[2]
    top_k = routes.shape[2]
    capacity = positions * top_k // owners * 5 // 4
    part = ep_count * capacity
    everyone = ep_count * positions
    my_cp = lax.axis_index("cp")
    my_ep = lax.axis_index("ep")
    gate_matrix = w_gate[0]
    up_matrix = w_up[0]
    down_matrix = w_down[0]

    meta = jnp.concatenate([routes[0].astype(F32), router_weights[0]], axis=1)
    meta = lax.all_gather(meta, "ep", axis=0, tiled=False)
    tok_all = lax.all_gather(tokens[0], "ep", axis=0, tiled=True)
    cot_all = lax.all_gather(cotangent[0], "ep", axis=0, tiled=True)

    def partner(step):
        return lax.rem(my_cp + step, cp_count)

    def out_to(step, value):
        return lax.ppermute(value, "cp", [(c, (c + step) % cp_count) for c in range(cp_count)])

    def back_from(step, value):
        return lax.ppermute(value, "cp", [((c + step) % cp_count, c) for c in range(cp_count)])

    all_routes = meta[:, :, :top_k].astype(jnp.int32)
    all_weights = meta[:, :, top_k:]
    earlier = (jnp.arange(positions)[:, None] < jnp.arange(positions)[None, :]).astype(F32)
    names, slots, weights = [], [], []
    for step in range(cp_count):
        expert = partner(step) * ep_count + my_ep
        named = all_routes == expert
        named_any = jnp.any(named, axis=2)
        rank = dot(named_any.astype(F32), earlier).astype(jnp.int32)
        base = jnp.arange(ep_count, dtype=jnp.int32)[:, None] * capacity
        slots.append(jnp.where(named_any, base + rank, -1).reshape(1, everyone))
        weights.append(jnp.sum(jnp.where(named, all_weights, 0.0), axis=2).reshape(everyone, 1))
        names.append(named)
    row_ids = jnp.arange(part, dtype=jnp.int32)
    pick = [row_ids[:, None] == slot for slot in slots]

    def pack(dense):
        return [dot(p.astype(BF16), dense).astype(BF16) for p in pick]

    def dispatch(packed):
        return [packed[0]] + [out_to(s, packed[s]) for s in range(1, cp_count)]

    arrived = dispatch(pack(tok_all))
    arrived, cot_packed = lax.optimization_barrier((arrived, pack(cot_all)))
    inputs = jnp.concatenate(arrived, axis=0)
    grad_in = jnp.concatenate(dispatch(cot_packed), axis=0)

    gate_pre = dot(inputs, gate_matrix)
    up_pre = dot(inputs, up_matrix)
    sig_gate = jax.nn.sigmoid(gate_pre)
    silu_gate = gate_pre * sig_gate
    hidden = (silu_gate * up_pre).astype(BF16)
    expert_out = dot(hidden, down_matrix).astype(BF16)

    spread = []
    for step in range(cp_count):
        here = row_ids[None, :] == slots[step].reshape(everyone, 1)
        spread.append(jnp.where(here, weights[step], 0.0))
    spread = jnp.concatenate(spread, axis=1)
    spread_hi = lax.reduce_precision(spread, 8, 7)
    spread_lo = (spread - spread_hi).astype(BF16)
    spread_hi = spread_hi.astype(BF16)

    def bring_back(rows):
        pieces = [rows[s * part:(s + 1) * part] for s in range(cp_count)]
        return [pieces[0]] + [back_from(s, pieces[s]) for s in range(1, cp_count)]

    def combine(pieces):
        rows = jnp.concatenate(pieces, axis=0)
        dense = (dot(spread_hi, rows) + dot(spread_lo, rows)).astype(BF16)
        return lax.psum_scatter(dense, "ep", scatter_dimension=0, tiled=True)

    out_pieces = bring_back(expert_out)

    grad_hidden = dot(grad_in, down_matrix, (1, 1))
    grad_gate = (grad_hidden * up_pre * sig_gate * (1.0 + gate_pre * (1.0 - sig_gate))).astype(BF16)
    grad_up = (grad_hidden * silu_gate).astype(BF16)
    expert_grad = (
        dot(grad_gate, gate_matrix, (1, 1)) + dot(grad_up, up_matrix, (1, 1))
    ).astype(BF16)
    grad_pieces = bring_back(expert_grad)

    layer_out = combine(out_pieces)
    gate_parts = jnp.zeros((ep_count, positions, top_k), F32)
    for step in range(cp_count):
        scores = jnp.sum(
            cot_packed[step].astype(F32) * out_pieces[step].astype(F32), axis=1, keepdims=True
        )
        by_token = jnp.sum(jnp.where(pick[step], scores, 0.0), axis=0)
        gate_parts += jnp.where(names[step], by_token.reshape(ep_count, positions, 1), 0.0)
    gate_grad = lax.psum_scatter(gate_parts, "ep", scatter_dimension=0, tiled=False)
    token_grad = combine(grad_pieces)
    return layer_out[None], token_grad[None], gate_grad[None]


def solution(mesh):
    in_specs = (
        P("ep", "cp", None),
        P("ep", "cp", None),
        P("ep", "cp", None),
        P("ep", "cp", None),
        P(("cp", "ep"), None, None),
        P(("cp", "ep"), None, None),
        P(("cp", "ep"), None, None),
    )
    out_specs = (P("ep", "cp", None), P("ep", "cp", None), P("ep", "cp", None))
    return jax.shard_map(
        per_device, mesh=mesh, in_specs=in_specs, out_specs=out_specs, check_vma=False
    )
```
